32 devices in a mesh: seq: 4 (over x, core), exp: 8 (over z, y).
Axes of the slice: x: 2, y: 2, z: 4, core: 2. Of those that a mesh axis runs over, the one named last changes fastest.
Arguments:
- xin: bfloat16 [256, 4, 8192], P('seq', None, 'exp'), may hold values from -6 to 6
- zin: bfloat16 [256, 4, 8192], P('seq', None, 'exp'), may hold values from -6 to 6
- conv_weight: float32 [4, 8192], P(None, 'exp'), may hold values from -3 to 3
- conv_bias: float32 [8192], P('exp'), may hold values from -3 to 3
- xproj_weight: bfloat16 [8192, 288], P('exp'), may hold values from -0.0625 to 0.0625
- dtproj_weight: bfloat16 [256, 8192], P(None, 'exp'), may hold values from -0.375 to 0.375
- dt_bias: float32 [8192], P('exp'), may hold values from -5 to -3
- a_log: float32 [16, 8192], P(None, 'exp'), may hold values from -3 to 1
- skip: float32 [8192], P('exp'), may hold values from 0.2 to 1
- out_weight: bfloat16 [8192, 4096], P('exp'), may hold values from -0.0625 to 0.0625
- resid: bfloat16 [256, 4, 4096], P(('seq', 'exp')), may hold values from -6 to 6
- norm_gain: float32 [4096], replicated, may hold values from 0.5 to 1.5
- expert_ids: int32 [256, 4, 2], P(('seq', 'exp')), may hold values from 0 to 7, all different within a row; in each aligned block of 32 rows (0 to 31, 32 to 63, ..., all dimensions but the last counted through in order) at most 16 rows name the same one
- gate_weights: bfloat16 [256, 4, 2], P(('seq', 'exp')), may hold values from 0.19921875 to 1
- w_gate: bfloat16 [8, 4096, 12288], P('exp', None, 'seq'), may hold values from -0.09375 to 0.09375
- w_up: bfloat16 [8, 4096, 12288], P('exp', None, 'seq'), may hold values from -0.09375 to 0.09375
- w_down: bfloat16 [8, 12288, 4096], P('exp', 'seq'), may hold values from -0.0546875 to 0.0546875
Outputs:
- layer_out: bfloat16 [256, 4, 4096], P(('seq', 'exp'))
The draws below stay inside these ranges and needn't reach their ends.
Inputs may be any that keep to these rules, and one draw needn't show every extreme that they name: `expert_ids`: tokens are ordered by position, then document; in each aligned block of 32 such tokens (the tokens of one device), every expert is named at most 16 times, and in every draw some expert is named exactly 16 times in some block. Each token names 2 different experts.
All inputs are finite; a program needn't handle non-finite values.
Results may differ from the reference program's by a relative error of at most 0.03.
Values may be sent and summed in bfloat16 or wider, within the bound.
A program may use at most 192 MiB of HBM per device.

```python
import math
import jax
import jax.numpy as jnp
import numpy as np
from jax import lax

D = 4096
EI = 8192
STATE = 16
CONV = 4
RANK = 256
EXPERTS = 8
TOPK = 2
FF = 12288
SEQS = 4
LENGTH = 256
SPLITS = 1
FF_PART = 12288
ROWS = 32
CAP = 16
N_SEQ = 4
N_EXP = 8


def level_of(own_key, extent, cuts, smallest, high):
    loudness = 1.0
    for dim, blocks in cuts:
        steps = jax.random.uniform(jax.random.fold_in(jax.random.fold_in(own_key, 6), dim), (blocks,), jnp.float32, smallest / len(cuts), high / len(cuts))
        loudness = loudness * jnp.repeat(jnp.exp(steps), extent[dim] // blocks).reshape((-1,) + (1,) * (len(extent) - 1 - dim))
    return loudness


def shared_out(rng, own, number, rows, amount, top, reach, lean):
    ranking = jax.random.permutation(rng, amount)
    crowded, common = load_shares(amount, rows * top, reach, lean, True), load_shares(amount, rows * top, reach, lean, False)
    places = jnp.arange(amount)

    def named(sizes, rotation):
        used = int((sizes > 0).sum())
        fixed = max(1, used // 4)
        moved = fixed + (places - fixed + rotation * (used - fixed)) % max(1, amount - fixed)
        return jnp.zeros((amount,), jnp.int32).at[ranking[jnp.where(places < fixed, places, moved)]].set(jnp.asarray(sizes, jnp.int32))

    sizes = jnp.where(number % 4 == 0, named(crowded, number // 4), named(common, number - number // 4 - 1))
    mixed = jax.random.permutation(jax.random.fold_in(own, 3), amount)
    donor, taker = mixed[0:amount // 2 * 2:2], mixed[1:amount // 2 * 2:2]
    room = jnp.minimum(sizes[donor] - 1, reach - sizes[taker]) // 2
    room = jnp.where((donor == ranking[0]) | (taker == ranking[0]) | (sizes[taker] == 0), 0, jnp.maximum(room, 0))
    moved = jax.random.randint(jax.random.fold_in(own, 4), (amount // 2,), 0, 1 << 20) % (room + 1)
    sizes = sizes.at[donor].add(-moved).at[taker].add(moved)
    members = jnp.searchsorted(jnp.cumsum(sizes), jnp.arange(rows * top), side="right").astype(jnp.int32)
    listing = members.reshape(top, rows).T
    listing = listing[jax.random.permutation(jax.random.fold_in(own, 1), rows)]
    rotation = jax.random.randint(jax.random.fold_in(own, 2), (rows, 1), 0, top)
    return jnp.take_along_axis(listing, (jnp.arange(top)[None, :] + rotation) % top, axis=1)


def load_shares(amount, total, most, lean, full):
    loads = [(1 << 20) // math.isqrt(standing ** lean) + 1 for standing in range(1, amount + 1)]
    largest = most if full else min(most, max(-(-total // amount), total * loads[0] // sum(loads)))
    least = 1 if total - largest >= amount - 1 else 0
    holding, rest = [largest] + [least] * (amount - 1), total - largest - least * (amount - 1)
    while rest > 0:
        candidates = [i for i in range(1, amount) if holding[i] < largest] or [i for i in range(1, amount) if holding[i] < most]
        whole, left = sum([loads[i] for i in candidates]), rest
        for i in candidates:
            more = min(most - holding[i], max(1, left * loads[i] // whole), rest)
            holding[i] = holding[i] + more
            rest = rest - more
    return np.array(holding)


def scatter_about(own_key, extent, scale, reach, pieces=(), kind=jnp.bfloat16):
    values = jax.random.normal(own_key, extent, jnp.float32) * scale
    if len(pieces) > 0:
        values = level_of(own_key, extent, pieces, -0.22, 0.18) * values
    return jnp.clip(values, min=-reach, max=reach).astype(kind)


def setup_inputs(seed: int = 0) -> dict:
    splits = jax.random.split(jax.random.key(seed), 18)
    xin = scatter_about(splits[0], (LENGTH, SEQS, EI), 1.0, 6.0, ((0, 4), (2, 8)))
    zin = scatter_about(splits[1], (LENGTH, SEQS, EI), 1.0, 6.0, ((0, 4), (2, 8)))
    conv_weight = scatter_about(splits[2], (CONV, EI), 0.5, 3.0, ((1, 8),), jnp.float32)
    conv_bias = scatter_about(splits[3], (EI,), 0.5, 3.0, ((0, 8),), jnp.float32)
    xproj_weight = scatter_about(splits[4], (EI, RANK + 2 * STATE), EI ** -0.5, 0.0625, ((0, 8),))
    dtproj_weight = scatter_about(splits[5], (RANK, EI), RANK ** -0.5, 0.375, ((1, 8),))
    dt_bias = jnp.clip(-5.0 + 2.0 * jax.random.uniform(splits[6], (EI,), jnp.float32) ** level_of(splits[6], (EI,), ((0, 8),), -0.2, 0.2), -5.0, -3.0)
    a_log = jnp.clip(-3.0 + 4.0 * jax.random.uniform(splits[7], (STATE, EI), jnp.float32) ** level_of(splits[7], (STATE, EI), ((1, 8),), -0.2, 0.2), -3.0, 1.0)
    skip = jnp.clip(0.2 + 0.8 * jax.random.uniform(splits[8], (EI,), jnp.float32) ** level_of(splits[8], (EI,), ((0, 8),), -0.2, 0.2), 0.2, 1.0)
    out_weight = scatter_about(splits[9], (EI, D), EI ** -0.5, 0.0625, ((0, 8),))
    resid = scatter_about(splits[10], (LENGTH, SEQS, D), 1.0, 6.0, ((0, 32),))
    norm_gain = jnp.clip(1.0 + 0.1 * jax.random.normal(splits[11], (D,), jnp.float32), 0.5, 1.5)
    expert_ids_keys = jax.random.split(jax.random.fold_in(splits[12], 1), LENGTH * SEQS // ROWS)
    expert_ids_turns = jax.random.permutation(jax.random.fold_in(splits[12], 3), LENGTH * SEQS // ROWS)
    expert_ids = jax.vmap(lambda own, number: shared_out(jax.random.fold_in(splits[12], 2), own, number, ROWS, EXPERTS, TOPK, CAP, 2))(expert_ids_keys, expert_ids_turns).reshape((LENGTH, SEQS, TOPK))
    gate_weights = jnp.clip(0.19921875 + 0.80078125 * jax.random.uniform(splits[13], (LENGTH, SEQS, TOPK), jnp.float32) ** level_of(splits[13], (LENGTH, SEQS, TOPK), ((0, 32),), -0.2, 0.2), 0.19921875, 1.0).astype(jnp.bfloat16)
    w_gate = scatter_about(splits[14], (N_EXP, D, FF_PART), D ** -0.5, 0.09375, ((0, 8), (2, 4)))
    w_up = scatter_about(splits[15], (N_EXP, D, FF_PART), D ** -0.5, 0.09375, ((0, 8), (2, 4)))
    w_down = scatter_about(splits[16], (N_EXP, FF_PART, D), FF ** -0.5, 0.0546875, ((0, 8), (1, 4)))
    return {"xin": xin, "zin": zin, "conv_weight": conv_weight, "conv_bias": conv_bias, "xproj_weight": xproj_weight, "dtproj_weight": dtproj_weight, "dt_bias": dt_bias, "a_log": a_log, "skip": skip, "out_weight": out_weight, "resid": resid, "norm_gain": norm_gain, "expert_ids": expert_ids, "gate_weights": gate_weights, "w_gate": w_gate, "w_up": w_up, "w_down": w_down}


def conv_inputs(window, conv_weight, conv_bias, length):
    running = jnp.zeros(window[:length].shape, jnp.float32) + conv_bias
    for offset in range(CONV):
        running = running + conv_weight[offset] * window[offset:offset + length]
    return running

def make_step(decay_rate):

    def advance(carry_state, series_now):
        step_now, input_now, read_now, value_now = series_now
        factor = jnp.exp(step_now[:, None, :] * decay_rate[None])
        carry_state = factor * carry_state + (step_now * value_now)[:, None, :] * input_now[:, :, None]
        return (carry_state, lax.optimization_barrier(jnp.sum(read_now[:, :, None] * carry_state, axis=1)))
    return advance

def slot_select(route_ids, capacity):
    flat_ids = route_ids.reshape(-1)
    onehot = (flat_ids[:, None] == jnp.arange(EXPERTS, dtype=jnp.int32)[None, :]).astype(jnp.int32)
    before = lax.optimization_barrier(jnp.sum((jnp.cumsum(onehot, axis=0) - onehot) * onehot, axis=1))
    target = flat_ids * capacity + before
    matches = jnp.arange(EXPERTS * capacity, dtype=jnp.int32)[:, None] == target[None, :]
    return matches.reshape(EXPERTS * capacity, route_ids.shape[0], route_ids.shape[1])

def reference(xin, zin, conv_weight, conv_bias, xproj_weight, dtproj_weight, dt_bias, a_log, skip, out_weight, resid, norm_gain, expert_ids, gate_weights, w_gate, w_up, w_down):
    xf = xin.astype(jnp.float32)
    window = jnp.concatenate([jnp.zeros((CONV - 1,) + xf.shape[1:], jnp.float32), xf], axis=0)
    inner_act = jax.nn.silu(conv_inputs(window, conv_weight, conv_bias, LENGTH)).astype(jnp.bfloat16)
    inner_f = inner_act.astype(jnp.float32)
    projected = jnp.einsum('pbc,cr->pbr', inner_f, xproj_weight.astype(jnp.float32))
    low_rank = projected[..., :RANK].astype(jnp.bfloat16)
    in_state = projected[..., RANK:RANK + STATE]
    out_state = projected[..., RANK + STATE:]
    step_size = jax.nn.softplus(jnp.einsum('pbr,rc->pbc', low_rank.astype(jnp.float32), dtproj_weight.astype(jnp.float32)) + dt_bias)
    decay_rate = -jnp.exp(a_log)
    zero_state = jnp.zeros((SEQS, STATE, EI), jnp.float32)
    ignored, ssm_out = lax.scan(make_step(decay_rate), zero_state, (step_size, in_state, out_state, inner_f))
    mixed_in = ((ssm_out + skip * inner_f) * jax.nn.silu(zin.astype(jnp.float32))).astype(jnp.bfloat16)
    hidden_state = resid.astype(jnp.float32) + jnp.einsum('pbc,cd->pbd', mixed_in.astype(jnp.float32), out_weight.astype(jnp.float32))
    norm_scale = lax.rsqrt(lax.optimization_barrier(jnp.mean(hidden_state * hidden_state, axis=-1, keepdims=True)) + 1e-05)
    normed = (hidden_state * norm_scale * norm_gain).astype(jnp.bfloat16)
    tokens = normed.reshape(-1, ROWS, D)
    route_ids = expert_ids.reshape(-1, ROWS, TOPK)
    gate_vals = gate_weights.astype(jnp.float32).reshape(-1, ROWS, TOPK)
    matches = jax.vmap(lambda block_ids: slot_select(block_ids, CAP))(route_ids)
    chosen = lax.optimization_barrier(jnp.sum(matches.astype(jnp.float32), axis=3))
    buffer = jnp.einsum('nqr,nrd->qnd', chosen, tokens.astype(jnp.float32), precision=lax.Precision.HIGHEST).astype(jnp.bfloat16)
    buffer = buffer.reshape(EXPERTS, -1, D)
    part_width = FF_PART // N_SEQ

    def run_expert(expert):
        row_block = buffer[expert]
        running = jnp.zeros(row_block.shape, jnp.float32)
        for split_index in range(SPLITS):
            gate_full = w_gate[split_index * EXPERTS + expert]
            up_full = w_up[split_index * EXPERTS + expert]
            down_full = w_down[split_index * EXPERTS + expert]
            for part_index in range(N_SEQ):
                low = part_index * part_width
                gate_act = jnp.dot(row_block, gate_full[:, low:low + part_width], preferred_element_type=jnp.float32)
                up_act = jnp.dot(row_block, up_full[:, low:low + part_width], preferred_element_type=jnp.float32)
                hidden = (jax.nn.silu(gate_act) * up_act).astype(jnp.bfloat16)
                term = jnp.dot(hidden, down_full[low:low + part_width], preferred_element_type=jnp.float32).astype(jnp.bfloat16)
                running = running + term.astype(jnp.float32)
        return running
    results = lax.map(run_expert, jnp.arange(EXPERTS, dtype=jnp.int32))
    results = results.reshape(EXPERTS * CAP, -1, D)
    weights = lax.optimization_barrier(jnp.sum(matches.astype(jnp.float32) * gate_vals[:, None, :, :], axis=3))
    expert_out = jnp.einsum('nqr,qnd->nrd', weights, results, precision=lax.Precision.HIGHEST)
    return (hidden_state + expert_out.reshape(hidden_state.shape)).astype(jnp.bfloat16)
```

```python
import functools

import jax
import jax.numpy as jnp
from jax import lax
from jax.experimental import pallas as pl
from jax.experimental.pallas import tpu as pltpu
from jax.sharding import PartitionSpec as P

D = 4096
STATE = 16
CONV = 4
RANK = 256
EXPERTS = 8
TOPK = 2


def passed_along(value, axis, by):
    count = lax.axis_size(axis)
    pairs = [(i, i + by) for i in range(count) if 0 <= i + by < count]
    return lax.ppermute(value, axis, pairs)


def conv_inputs(window, conv_weight, conv_bias, length):
    running = jnp.zeros(window[:length].shape, jnp.float32) + conv_bias
    for offset in range(CONV):
        running = running + conv_weight[offset] * window[offset : offset + length]
    return running


MESH = pl.DeviceIdType.MESH
VMEM = pl.BlockSpec(memory_space=pltpu.VMEM)


def remote(src, dst, send, recv, where):
    return pltpu.make_async_remote_copy(
        src_ref=src,
        dst_ref=dst,
        send_sem=send,
        recv_sem=recv,
        device_id=where,
        device_id_type=MESH,
    )


def greet(others):
    barrier = pltpu.get_barrier_semaphore()
    for other in others:
        pl.semaphore_signal(barrier, inc=1, device_id=other, device_id_type=MESH)
    pl.semaphore_wait(barrier, len(others))


def total_of(first, rest):
    total = first.astype(jnp.float32)
    for value in rest:
        total = total + value.astype(jnp.float32)
    return total


def communicating(kernel, number, out, scratch, operand):
    return pl.pallas_call(
        kernel,
        out_shape=out,
        in_specs=[VMEM],
        out_specs=VMEM,
        scratch_shapes=scratch,
        compiler_params=pltpu.CompilerParams(
            collective_id=number, has_side_effects=True, vmem_limit_bytes=40 * 2**20
        ),
    )(operand)


def dma(count):
    return pltpu.SemaphoreType.DMA((count,))


def sum_kernel(n, x, out, arrived, spread, send1, recv1, send2, recv2):
    row, me = lax.axis_index("seq"), lax.axis_index("exp")
    greet([(row, lax.rem(me + k, n)) for k in range(1, n)])
    copies = []
    for k in range(1, n):
        peer = lax.rem(me + k, n)
        copies.append(
            remote(x.at[peer], arrived.at[k - 1], send1.at[k - 1], recv1.at[k - 1], (row, peer))
        )
        copies[-1].start()
    for copy in copies:
        copy.wait_recv()
    spread[me] = total_of(x[me], [arrived[k] for k in range(n - 1)]).astype(jnp.bfloat16)
    again = []
    for k in range(1, n):
        peer = lax.rem(me + k, n)
        again.append(
            remote(spread.at[me], spread.at[me], send2.at[k - 1], recv2.at[k - 1], (row, peer))
        )
        again[-1].start()
    for copy in again:
        copy.wait_recv()
    out[...] = spread[...]
    for copy in copies + again:
        copy.wait_send()


def summed_over_exp(value):
    n = lax.axis_size("exp")
    rows, columns = value.shape
    blocks = value.reshape(n, rows // n, columns)
    return communicating(
        functools.partial(sum_kernel, n),
        0,
        jax.ShapeDtypeStruct(blocks.shape, jnp.bfloat16),
        [
            pltpu.VMEM((n - 1,) + blocks.shape[1:], jnp.bfloat16),
            pltpu.VMEM(blocks.shape, jnp.bfloat16),
        ]
        + [dma(n - 1)] * 4,
        blocks,
    ).reshape(rows, columns)


def scatter_kernel(outer, inner, parts, x, out, first, middle, second, send1, recv1, send2, recv2):
    row, me = lax.axis_index("seq"), lax.axis_index("exp")
    o, i = me // inner, lax.rem(me, inner)
    near = [lax.rem(i + d, inner) for d in range(1, inner)]
    far = [lax.rem(o + d, outer) for d in range(1, outer)]
    greet([(row, o * inner + p) for p in near] + [(row, p * inner + i) for p in far])
    width = x.shape[3] // parts
    ones, twos = [], []
    for c in range(parts):
        columns = pl.ds(c * width, width)
        ones.append([])
        for d, p in enumerate(near):
            at = c * len(near) + d
            ones[c].append(
                remote(
                    x.at[:, p, :, columns],
                    first.at[d, :, :, columns],
                    send1.at[at],
                    recv1.at[at],
                    (row, o * inner + p),
                )
            )
            ones[c][d].start()
    for c in range(parts):
        columns = pl.ds(c * width, width)
        for copy in ones[c]:
            copy.wait_recv()
        for q in range(outer):
            middle[q, :, columns] = total_of(
                x[q, i, :, columns], [first[d, q, :, columns] for d in range(len(near))]
            ).astype(jnp.bfloat16)
        twos.append([])
        for d, p in enumerate(far):
            at = c * len(far) + d
            twos[c].append(
                remote(
                    middle.at[p, :, columns],
                    second.at[d, :, columns],
                    send2.at[at],
                    recv2.at[at],
                    (row, p * inner + i),
                )
            )
            twos[c][d].start()
    for c in range(parts):
        columns = pl.ds(c * width, width)
        for copy in twos[c]:
            copy.wait_recv()
        out[:, columns] = total_of(
            middle[o, :, columns], [second[d, :, columns] for d in range(len(far))]
        )
    for copy in sum(ones, []) + sum(twos, []):
        copy.wait_send()


def scattered_over_exp(value):
    n = lax.axis_size("exp")
    outer, parts = 4, 4
    inner = n // outer
    rows, columns = value.shape
    rows = rows // n
    near, far = parts * (inner - 1), parts * (outer - 1)
    return communicating(
        functools.partial(scatter_kernel, outer, inner, parts),
        1,
        jax.ShapeDtypeStruct((rows, columns), jnp.float32),
        [
            pltpu.VMEM((inner - 1, outer, rows, columns), jnp.bfloat16),
            pltpu.VMEM((outer, rows, columns), jnp.bfloat16),
            pltpu.VMEM((outer - 1, rows, columns), jnp.bfloat16),
            dma(near),
            dma(near),
            dma(far),
            dma(far),
        ],
        value.reshape(outer, inner, rows, columns),
    )


def places(n_seq, n_exp):
    row, me = lax.axis_index("seq"), lax.axis_index("exp")
    count = n_seq // 2
    chip, core = row // 2, lax.rem(row, 2)
    chips = [lax.rem(chip + d, count) for d in range(count)]
    back = [lax.rem(chip + count - d, count) for d in range(count)]
    partner = (chip * 2 + 1 - core, me)
    greet(
        [(row, lax.rem(me + k, n_exp)) for k in range(1, n_exp)]
        + [(p * 2 + core, me) for p in chips[1:]]
        + [partner]
    )
    return row, me, count, core, chips, back, partner


def dispatch_kernel(n_seq, n_exp, x, out, send1, recv1, send2, recv2, send3, recv3):
    row, me, count, core, chips, back, partner = places(n_seq, n_exp)
    out[row, me] = x[me]
    ones, twos, threes = [], [], []
    for k in range(1, n_exp):
        peer = lax.rem(me + k, n_exp)
        ones.append(
            remote(x.at[peer], out.at[row, me], send1.at[k - 1], recv1.at[k - 1], (row, peer))
        )
        ones[-1].start()

    def shared(origin, source, at):
        block = out.at[origin, source]
        threes.append(remote(block, block, send3.at[at], recv3.at[at], partner))
        threes[-1].start()

    for k in range(n_exp):
        if k > 0:
            ones[k - 1].wait_recv()
        source = lax.rem(me + n_exp - k, n_exp)
        block = out.at[row, source]
        for d in range(1, count):
            at = (d - 1) * n_exp + k
            twos.append(
                remote(block, block, send2.at[at], recv2.at[at], (chips[d] * 2 + core, me))
            )
            twos[-1].start()
        shared(row, source, k)
    for k in range(n_exp):
        source = lax.rem(me + n_exp - k, n_exp)
        for d in range(1, count):
            twos[k * (count - 1) + d - 1].wait_recv()
            shared(back[d] * 2 + core, source, d * n_exp + k)
    for copy in threes:
        copy.wait_recv()
    for copy in ones + twos + threes:
        copy.wait_send()


def dispatched(value):
    n_seq, n_exp = lax.axis_size("seq"), lax.axis_size("exp")
    count = n_seq // 2
    across = (count - 1) * n_exp
    return communicating(
        functools.partial(dispatch_kernel, n_seq, n_exp),
        2,
        jax.ShapeDtypeStruct((n_seq,) + value.shape, jnp.bfloat16),
        [dma(n_exp - 1)] * 2 + [dma(across)] * 2 + [dma(count * n_exp)] * 2,
        value,
    )


def return_kernel(
    n_seq, n_exp, x, out, near, pair, far, total, send1, recv1, send2, recv2, send3, recv3
):
    row, me, count, core, chips, back, partner = places(n_seq, n_exp)
    order = list(range(1, n_exp)) + [0]
    targets = [lax.rem(me + k, n_exp) for k in order]
    ones, twos, threes = [], [], []
    for s in range(n_exp):
        ones.append([])
        for d in range(count):
            at = s * count + d
            ones[s].append(
                remote(
                    x.at[chips[d] * 2 + 1 - core, targets[s]],
                    near.at[chips[d], targets[s]],
                    send1.at[at],
                    recv1.at[at],
                    partner,
                )
            )
            ones[s][d].start()
    for s in range(n_exp + 1):
        if s < n_exp:
            twos.append([])
            for d in list(range(1, count)) + [0]:
                ones[s][d].wait_recv()
                place = (chips[d], targets[s])
                pair[place] = total_of(
                    x[chips[d] * 2 + core, targets[s]], [near[place]]
                ).astype(jnp.bfloat16)
                if d > 0:
                    at = s * (count - 1) + d - 1
                    twos[s].append(
                        remote(
                            pair.at[place],
                            far.at[d - 1, targets[s]],
                            send2.at[at],
                            recv2.at[at],
                            (chips[d] * 2 + core, me),
                        )
                    )
                    twos[s][-1].start()
        if s > 0:
            t = s - 1
            for copy in twos[t]:
                copy.wait_recv()
            block = total_of(
                pair[chips[0], targets[t]], [far[d, targets[t]] for d in range(count - 1)]
            ).astype(jnp.bfloat16)
            if order[t] == 0:
                out[me] = block
            else:
                total[targets[t]] = block
                threes.append(
                    remote(
                        total.at[targets[t]],
                        out.at[me],
                        send3.at[t],
                        recv3.at[t],
                        (row, targets[t]),
                    )
                )
                threes[-1].start()
    for copy in threes:
        copy.wait_recv()
    for copy in sum(ones, []) + sum(twos, []) + threes:
        copy.wait_send()


def sent_back(value):
    n_seq, n_exp = lax.axis_size("seq"), lax.axis_size("exp")
    count = n_seq // 2
    block = value.shape[1:]
    return communicating(
        functools.partial(return_kernel, n_seq, n_exp),
        3,
        jax.ShapeDtypeStruct(block, jnp.bfloat16),
        [
            pltpu.VMEM((count,) + block, jnp.bfloat16),
            pltpu.VMEM((count,) + block, jnp.bfloat16),
            pltpu.VMEM((count - 1,) + block, jnp.bfloat16),
            pltpu.VMEM(block, jnp.bfloat16),
        ]
        + [dma(count * n_exp)] * 2
        + [dma((count - 1) * n_exp)] * 2
        + [dma(n_exp - 1)] * 2,
        value,
    )


def scan_kernel(step, given, feed, decay, *rest):
    start, read, result = rest if len(rest) == 3 else (None, None, rest[0])
    wide = step.shape[2]
    rates = decay[...]

    def across(tile):
        return jnp.concatenate([tile] * (wide // 128), axis=1)

    def eight(block, state):
        rows = pl.ds(pl.multiple_of(block * 8, 8), 8)
        steps, values = step[0, rows, :], given[0, rows, :]
        outs = []
        for r in range(8):
            state = jnp.exp(steps[r : r + 1] * rates) * state + values[r : r + 1] * across(
                feed[0, block * 8 + r]
            )
            if read is not None:
                outs.append(
                    jnp.sum(across(read[0, block * 8 + r]) * state, axis=0, keepdims=True)
                )
        if read is not None:
            result[0, rows, :] = jnp.concatenate(outs, axis=0)
        return state

    first = jnp.zeros(rates.shape, jnp.float32) if start is None else start[0]
    last = lax.fori_loop(0, step.shape[1] // 8, eight, first)
    if read is None:
        result[0] = last


def run_scan(step, given, feed, decay, start=None, read=None):
    docs, length, channels = step.shape
    wide = 512
    series = pl.BlockSpec((1, length, wide), lambda b, c: (b, 0, c))
    states = pl.BlockSpec((1, length, STATE, 128), lambda b, c: (b, 0, 0, 0))
    rates = pl.BlockSpec((STATE, wide), lambda b, c: (0, c))
    whole = pl.BlockSpec((1, STATE, wide), lambda b, c: (b, 0, c))
    operands, specs = [step, given, feed, decay], [series, series, states, rates]
    if read is None:
        shape, out = (docs, STATE, channels), whole
    else:
        operands, specs = operands + [start, read], specs + [whole, states]
        shape, out = step.shape, series
    return pl.pallas_call(
        scan_kernel,
        grid=(docs, channels // wide),
        out_shape=jax.ShapeDtypeStruct(shape, jnp.float32),
        in_specs=specs,
        out_specs=out,
        compiler_params=pltpu.CompilerParams(vmem_limit_bytes=32 * 2**20),
    )(*operands)


def slot_select(route_ids, capacity):
    flat_ids = route_ids.reshape(-1)
    onehot = (flat_ids[:, None] == jnp.arange(EXPERTS, dtype=jnp.int32)[None, :]).astype(jnp.int32)
    before = jnp.sum((jnp.cumsum(onehot, axis=0) - onehot) * onehot, axis=1)
    target = flat_ids * capacity + before
    matches = jnp.arange(EXPERTS * capacity, dtype=jnp.int32)[:, None] == target[None, :]
    return matches.reshape(EXPERTS * capacity, route_ids.shape[0], route_ids.shape[1])


def per_device(
    xin,
    zin,
    conv_weight,
    conv_bias,
    xproj_weight,
    dtproj_weight,
    dt_bias,
    a_log,
    skip,
    out_weight,
    resid,
    norm_gain,
    expert_ids,
    gate_weights,
    w_gate,
    w_up,
    w_down,
):
    section = xin.shape[0]
    edge_rows = passed_along(xin[section - (CONV - 1) :], "seq", 1)
    window = jnp.concatenate([edge_rows, xin], axis=0).astype(jnp.float32)
    inner_act = jax.nn.silu(conv_inputs(window, conv_weight, conv_bias, section)).astype(
        jnp.bfloat16
    )
    inner_f = inner_act.astype(jnp.float32)
    docs, channels = xin.shape[1], xin.shape[2]
    count = section * docs
    padded = jnp.pad(xproj_weight, ((0, 0), (0, -xproj_weight.shape[1] % 128)))
    projected = jnp.dot(
        inner_act.reshape(count, channels), padded, preferred_element_type=jnp.float32
    )
    projected = summed_over_exp(projected.astype(jnp.bfloat16))
    projected = projected.reshape(section, docs, -1).transpose(1, 0, 2)
    low_rank = projected[..., :RANK]
    states = projected[..., RANK : RANK + 2 * STATE].astype(jnp.float32)
    spread = jnp.broadcast_to(states[..., None], states.shape + (128,))
    in_state, out_state = spread[:, :, :STATE], spread[:, :, STATE:]
    inner_t = inner_f.transpose(1, 0, 2)
    step_size = jax.nn.softplus(
        jnp.einsum("bpr,rc->bpc", low_rank, dtproj_weight, preferred_element_type=jnp.float32)
        + dt_bias
    )
    decay_rate = -jnp.exp(a_log)
    given = step_size * inner_t
    final_local = run_scan(step_size, given, in_state, decay_rate)
    all_steps = lax.all_gather(jnp.sum(step_size, axis=1), "seq")
    all_finals = lax.all_gather(final_local.astype(jnp.bfloat16), "seq")
    place = lax.axis_index("seq")
    incoming = jnp.zeros_like(final_local)
    for q in range(lax.axis_size("seq") - 1):
        through = jnp.exp(all_steps[q][:, None, :] * decay_rate[None])
        incoming = jnp.where(
            q < place, through * incoming + all_finals[q].astype(jnp.float32), incoming
        )
    ssm_out = run_scan(step_size, given, in_state, decay_rate, incoming, out_state)
    mixed_in = (
        (ssm_out.transpose(1, 0, 2) + skip * inner_f) * jax.nn.silu(zin.astype(jnp.float32))
    ).astype(jnp.bfloat16)
    mamba_rows = scattered_over_exp(
        jnp.dot(
            mixed_in.reshape(count, channels), out_weight, preferred_element_type=jnp.float32
        ).astype(jnp.bfloat16)
    ).reshape(resid.shape)
    hidden_state = resid.astype(jnp.float32) + mamba_rows
    norm_scale = lax.rsqrt(jnp.mean(hidden_state * hidden_state, axis=-1, keepdims=True) + 1e-05)
    normed = (hidden_state * norm_scale * norm_gain).astype(jnp.bfloat16)
    row_count = resid.shape[0] * resid.shape[1]
    capacity = 2 * TOPK * row_count // EXPERTS
    splits = lax.axis_size("exp") // EXPERTS
    tokens = normed.reshape(row_count, D)
    route_ids = expert_ids.reshape(row_count, TOPK)
    gate_vals = gate_weights.reshape(row_count, TOPK)
    matches = slot_select(route_ids, capacity)
    chosen = jnp.sum(matches.astype(jnp.int32), axis=2).astype(jnp.bfloat16)
    outgoing = (
        jnp.dot(chosen, tokens, preferred_element_type=jnp.float32)
        .astype(jnp.bfloat16)
        .reshape(EXPERTS, capacity, D)
    )
    row_block = dispatched(jnp.tile(outgoing, (splits, 1, 1)))
    expert_row_block = row_block.reshape(-1, D)
    gate_act = jnp.dot(expert_row_block, w_gate[0], preferred_element_type=jnp.float32)
    up_act = jnp.dot(expert_row_block, w_up[0], preferred_element_type=jnp.float32)
    hidden = (jax.nn.silu(gate_act) * up_act).astype(jnp.bfloat16)
    returned = sent_back(
        jnp.dot(hidden, w_down[0], preferred_element_type=jnp.float32)
        .astype(jnp.bfloat16)
        .reshape(row_block.shape)
    ).astype(jnp.float32)
    summed = jnp.sum(returned.reshape(splits, EXPERTS * capacity, D), axis=0)
    weights = jnp.sum(matches.astype(jnp.float32) * gate_vals.astype(jnp.float32)[None], axis=2)
    expert_out = jnp.dot(weights.T, summed, precision=lax.Precision.HIGHEST)
    return (hidden_state + expert_out.reshape(hidden_state.shape)).astype(jnp.bfloat16)


def solution(mesh):
    placed = (
        P("seq", None, "exp"),
        P("seq", None, "exp"),
        P(None, "exp"),
        P("exp"),
        P("exp", None),
        P(None, "exp"),
        P("exp"),
        P(None, "exp"),
        P("exp"),
        P("exp", None),
        P(("seq", "exp"), None, None),
        P(),
        P(("seq", "exp"), None, None),
        P(("seq", "exp"), None, None),
        P("exp", None, "seq"),
        P("exp", None, "seq"),
        P("exp", "seq", None),
    )
    return jax.shard_map(
        per_device,
        mesh=mesh,
        in_specs=placed,
        out_specs=P(("seq", "exp"), None, None),
        check_vma=False,
    )
```
